512 devices in a mesh: alpha: 32 (over x, z), beta: 16 (over y, core).
Axes of the slice: x: 4, y: 8, z: 8, core: 2. Of those that a mesh axis runs over, the one named last changes fastest.
Arguments:
- coeffs: bfloat16 [8192, 16384], P('alpha', 'beta'), may hold values from -6 to 6
- a_blocks: bfloat16 [2, 8192, 11, 128], P(None, 'alpha'), may hold values from -0.15625 to 0.15625
- a_list: int32 [2, 64, 11], replicated, may hold values from 0 to 63, as said below
- a_count: int32 [2, 64], replicated, may hold values from 4 to 11, as said below
- b_blocks: bfloat16 [2, 16384, 11, 128], P(None, 'beta'), may hold values from -0.15625 to 0.15625
- b_list: int32 [2, 128, 11], replicated, may hold values from 0 to 127, as said below
- b_count: int32 [2, 128], replicated, may hold values from 4 to 11, as said below
Outputs:
- sigma: float32 [8192, 16384], P('alpha', 'beta')
The draws below stay inside these ranges and needn't reach their ends.
Inputs may be any that keep to these rules, and one draw needn't show every extreme that they name: `a_list`: every entry, valid slot or not, is an alpha block number. For each index r of alpha and each index o of alpha, the entries of all operators in the rows of blocks r * 2 to r * 2 + 1 that lie in blocks o * 2 to o * 2 + 1 name at most 1 distinct blocks, and some pair names exactly 1. `b_list`: the same with beta, 8 and 2. `a_count`: some row has all 11 slots valid. `b_count`: some row has all 11 slots valid.
All inputs are finite; a program needn't handle non-finite values.
Results may differ from the reference program's by a relative error of at most 0.0029.
Values may be sent and summed in bfloat16 or wider, within the bound.
No kernel may reach another device: no remote copies, remote signals or barrier semaphores. Data moves between devices by JAX's collectives and lax.ppermute only.
A program may use at most 128 MiB of HBM per device.

```python
import jax
import jax.numpy as jnp
from jax import lax

BLOCK = 128
ABLK_DEV = 2
BBLK_DEV = 8
LIST = 11
OPS = 2
NA = 8192
NB = 16384
FROM_A = 1
FROM_B = 2
N_ALPHA = 32
N_BETA = 16


def listed_blocks(key, owners, per_owner, capacity):
    score_key = jax.random.fold_in(key, 101)
    pick_key = jax.random.fold_in(key, 202)
    scores = jax.random.randint(score_key, (owners, owners, per_owner), 0, 1 << 20)
    scores = scores * per_owner + jnp.arange(per_owner, dtype=jnp.int32)
    ordering = jnp.argsort(scores, axis=-1, stable=True)[..., :capacity].astype(jnp.int32)
    allowed = ordering + (jnp.arange(owners, dtype=jnp.int32) * per_owner)[None, :, None]
    allowed = allowed.reshape(owners, owners * capacity)
    picks = jax.random.randint(pick_key, (OPS, owners, per_owner, LIST), 0, owners * capacity)
    receivers = jnp.arange(owners, dtype=jnp.int32)[None, :, None, None]
    entries = allowed[receivers, picks]
    entries = entries.at[0, 0, 0, :capacity].set(allowed[0, :capacity])
    return entries.reshape(OPS, owners * per_owner, LIST).astype(jnp.int32)


def valid_counts(key, total):
    counts = jax.random.randint(key, (OPS, total), LIST // 3 + 1, LIST + 1)
    return counts.at[0, 0].set(LIST).astype(jnp.int32)


def draw_a_list(key, part):
    return listed_blocks(jax.random.fold_in(key, 11), N_ALPHA, ABLK_DEV, FROM_A)


def draw_b_list(key, part):
    return listed_blocks(jax.random.fold_in(key, 12), N_BETA, BBLK_DEV, FROM_B)


def draw_a_count(key, part):
    return valid_counts(jax.random.fold_in(key, 21), ABLK_DEV * N_ALPHA)


def draw_b_count(key, part):
    return valid_counts(jax.random.fold_in(key, 22), BBLK_DEV * N_BETA)


def level_of(own_key, dims, cuts, low, high):
    level, own = 1.0, jax.random.fold_in(own_key, 6)
    for position, blocks in cuts:
        steps = jnp.exp(jax.random.uniform(jax.random.fold_in(own, position), (blocks,), jnp.float32, low / len(cuts), high / len(cuts)))
        level = level * jnp.repeat(steps, dims[position] // blocks).reshape([-1 if axis == position else 1 for axis in range(len(dims))])
    return level


def centred(stream_key, dims, deviation, reach, cuts=(), kind=jnp.bfloat16):
    drawn = jax.random.normal(stream_key, dims, jnp.float32) * deviation
    if len(cuts) > 0:
        drawn = level_of(stream_key, dims, cuts, -0.22, 0.18) * drawn
    return jnp.clip(drawn, min=-reach, max=reach).astype(kind)


def setup_inputs(seed: int = 0) -> dict:
    seeds = jax.random.split(jax.random.key(seed), 8)
    coeffs = centred(seeds[0], (NA, NB), 1.0, 6.0, ((0, 32), (1, 16)))
    a_blocks = centred(seeds[1], (OPS, NA, LIST, BLOCK), (LIST * BLOCK) ** -0.5, 0.15625, ((1, 32),))
    a_list = draw_a_list(jax.random.fold_in(seeds[7], 71), 0)
    a_count = draw_a_count(jax.random.fold_in(seeds[7], 71), 0)
    b_blocks = centred(seeds[4], (OPS, NB, LIST, BLOCK), (LIST * BLOCK) ** -0.5, 0.15625, ((1, 16),))
    b_list = draw_b_list(jax.random.fold_in(seeds[7], 71), 0)
    b_count = draw_b_count(jax.random.fold_in(seeds[7], 71), 0)
    return {"coeffs": coeffs, "a_blocks": a_blocks, "a_list": a_list, "a_count": a_count, "b_blocks": b_blocks, "b_list": b_list, "b_count": b_count}


def reference(coeffs, a_blocks, a_list, a_count, b_blocks, b_list, b_count):
    operators, alpha_total, list_slots, block_size = a_blocks.shape
    beta_total = coeffs.shape[1]
    alpha_nblk = alpha_total // block_size
    beta_nblk = beta_total // block_size
    slot_ids = jnp.arange(list_slots, dtype=jnp.int32)
    coeff_blocks = coeffs.reshape(alpha_nblk, block_size, beta_total)
    sigma = jnp.zeros((alpha_total, beta_total), jnp.float32)
    for k in range(operators):
        alpha_valid = slot_ids[None, :] < a_count[k][:, None]
        alpha_kept = jnp.where(alpha_valid[:, None, :, None], a_blocks[k].reshape(alpha_nblk, block_size, list_slots, block_size), jnp.zeros((), a_blocks.dtype))

        def row_block(pair):
            factor_rows, entries = pair
            picked = coeff_blocks[entries.astype(jnp.int32)].reshape(list_slots * block_size, beta_total)
            return jnp.dot(factor_rows.reshape(block_size, list_slots * block_size), picked, preferred_element_type=jnp.float32)

        inter = lax.map(row_block, (alpha_kept, a_list[k]))
        inter = inter.reshape(alpha_total, beta_total).astype(jnp.bfloat16)
        inter_cols = inter.reshape(alpha_total, beta_nblk, block_size)
        beta_valid = slot_ids[None, :] < b_count[k][:, None]
        beta_kept = jnp.where(beta_valid[:, None, :, None], b_blocks[k].reshape(beta_nblk, block_size, list_slots, block_size), jnp.zeros((), b_blocks.dtype))

        def col_block(pair):
            factor_rows, entries = pair
            picked = inter_cols[:, entries.astype(jnp.int32), :].reshape(alpha_total, list_slots * block_size)
            return jnp.dot(picked, factor_rows.reshape(block_size, list_slots * block_size).T, preferred_element_type=jnp.float32)

        partial_sigma = lax.map(col_block, (beta_kept, b_list[k]))
        sigma = sigma + jnp.transpose(partial_sigma, (1, 0, 2)).reshape(alpha_total, beta_total)
    return sigma
```

```python
import functools

import jax
import jax.numpy as jnp
from jax import lax
from jax.experimental import pallas as pl
from jax.experimental.pallas import tpu as pltpu
from jax.sharding import PartitionSpec as P

X, Z = 4, 8
Y, CORES = 8, 2
NBETA = Y * CORES
BLK = 128
FROM_B = 2
VMEM_LIMIT = 40 * 1024 * 1024

Z_GROUPS = [[x * Z + z for z in range(Z)] for x in range(X)]
X_GROUPS = [[x * Z + z for x in range(X)] for z in range(Z)]


def shift_x(step):
    return [(x * Z + z, (x + step) % X * Z + z) for x in range(X) for z in range(Z)]


SWAP_CORES = [(y * CORES + c, y * CORES + 1 - c) for y in range(Y) for c in range(CORES)]


def params():
    return pltpu.CompilerParams(vmem_limit_bytes=VMEM_LIMIT)


def pack_kernel(wanted, c_ref, out_ref, sems):
    def each(action):
        for t in range(NBETA * FROM_B):
            column = pl.multiple_of(wanted[t] * BLK, BLK)
            copy = pltpu.make_async_copy(
                c_ref.at[:, pl.ds(column, BLK)], out_ref.at[t], sems.at[t]
            )
            action(copy)

    each(lambda copy: copy.start())
    each(lambda copy: copy.wait())


def pack(wanted, c):
    rows = c.shape[0]
    total = NBETA * FROM_B
    return pl.pallas_call(
        pack_kernel,
        grid_spec=pltpu.PrefetchScalarGridSpec(
            num_scalar_prefetch=1,
            grid=(1,),
            in_specs=[pl.BlockSpec(c.shape, lambda i, w: (0, 0))],
            out_specs=pl.BlockSpec(memory_space=pl.ANY),
            scratch_shapes=[pltpu.SemaphoreType.DMA((total,))],
        ),
        out_shape=jax.ShapeDtypeStruct((total, rows, BLK), c.dtype),
        compiler_params=params(),
        cost_estimate=pl.CostEstimate(flops=0, bytes_accessed=5 << 20, transcendentals=0),
        name="pack",
    )(wanted, c)


def sum_pack_kernel(wanted, parts_ref, out_ref, inter, sems):
    for b in range(inter.shape[0]):
        columns = slice(b * BLK, (b + 1) * BLK)
        total = parts_ref[0, :, columns].astype(jnp.float32)
        for x in range(1, X):
            total += parts_ref[x, :, columns].astype(jnp.float32)
        inter[b] = total.astype(inter.dtype)

    def each(action):
        for t in range(NBETA * FROM_B):
            action(pltpu.make_async_copy(inter.at[wanted[t]], out_ref.at[t], sems.at[t]))

    each(lambda copy: copy.start())
    each(lambda copy: copy.wait())


def sum_pack(wanted, parts):
    _, rows, cols = parts.shape
    total = NBETA * FROM_B
    return pl.pallas_call(
        sum_pack_kernel,
        grid_spec=pltpu.PrefetchScalarGridSpec(
            num_scalar_prefetch=1,
            grid=(1,),
            in_specs=[pl.BlockSpec(parts.shape, lambda i, w: (0, 0, 0))],
            out_specs=pl.BlockSpec(memory_space=pl.ANY),
            scratch_shapes=[
                pltpu.VMEM((cols // BLK, rows, BLK), jnp.bfloat16),
                pltpu.SemaphoreType.DMA((total,)),
            ],
        ),
        out_shape=jax.ShapeDtypeStruct((total, rows, BLK), jnp.bfloat16),
        compiler_params=params(),
        cost_estimate=pl.CostEstimate(flops=1 << 20, bytes_accessed=6 << 20, transcendentals=0),
        name="sum_pack",
    )(wanted, parts)


def beta_kernel(op, slots, place, pool_ref, b_ref, *rest):
    out_ref = rest[-1]
    block = pl.program_id(0)
    picked = [pool_ref[place[op, block, s]] for s in range(slots)]
    total = lax.dot_general(
        jnp.concatenate(picked, axis=1),
        b_ref[...],
        (((1,), (1,)), ((), ())),
        preferred_element_type=jnp.float32,
    )
    if len(rest) == 2:
        total += rest[0][...]
    out_ref[...] = total.astype(out_ref.dtype)


def beta_product(op, place, pool, b_flat, added, dtype):
    _, cols, depth = b_flat.shape
    rows = pool.shape[1]
    in_specs = [
        pl.BlockSpec(pool.shape, lambda i, p: (0, 0, 0)),
        pl.BlockSpec((None, BLK, depth), lambda i, p: (op, i, 0)),
    ]
    operands = [pool, b_flat]
    if added is not None:
        in_specs.append(pl.BlockSpec((rows, BLK), lambda i, p: (0, i)))
        operands.append(added)
    return pl.pallas_call(
        functools.partial(beta_kernel, op, depth // BLK),
        grid_spec=pltpu.PrefetchScalarGridSpec(
            num_scalar_prefetch=1,
            grid=(cols // BLK,),
            in_specs=in_specs,
            out_specs=pl.BlockSpec((rows, BLK), lambda i, p: (0, i)),
        ),
        out_shape=jax.ShapeDtypeStruct((rows, cols), dtype),
        compiler_params=params(),
        cost_estimate=pl.CostEstimate(
            flops=2 * rows * cols * depth, bytes_accessed=7 << 20, transcendentals=0
        ),
        name="beta_product",
    )(place, *operands)


def alpha_kernel(op, slots, block, core, place, pool_ref, own, near, far, *rest):
    out_ref, factors, total, sems = rest
    step = pl.program_id(0)

    def copy_of(source, t):
        return pltpu.make_async_copy(source, factors.at[t], sems.at[t])

    @pl.when(step == 0)
    def _():
        copy_of(own.at[op], 0).start()

        @pl.when(core[0] == op)
        def _():
            for t in range(1, X):
                copy_of(near.at[t - 1], t).start()

        @pl.when(core[0] != op)
        def _():
            for t in range(1, X):
                copy_of(far.at[t - 1], t).start()

    copy_of(own.at[op], step).wait()
    for b in range(block):
        rows = slice(b * BLK, (b + 1) * BLK)
        total[...] = jnp.zeros_like(total)
        for s in range(slots):
            chosen = place[op, step, b, s]

            @pl.when(chosen >= 0)
            def _():
                total[...] += jnp.dot(
                    factors[step, rows, s * BLK : (s + 1) * BLK],
                    pool_ref[chosen],
                    preferred_element_type=jnp.float32,
                )

        out_ref[rows, :] = total[...].astype(out_ref.dtype)


def alpha_partials(op, core, target, place, gathered, own, near, far, dtype):
    _, rows, depth = own.shape
    cols = gathered.shape[1]
    pool = gathered.reshape(gathered.shape[0] // BLK, BLK, cols)
    anywhere = pl.BlockSpec(memory_space=pl.ANY)
    return pl.pallas_call(
        functools.partial(alpha_kernel_entry, op, depth // BLK, rows // BLK),
        grid_spec=pltpu.PrefetchScalarGridSpec(
            num_scalar_prefetch=3,
            grid=(X,),
            in_specs=[
                pl.BlockSpec(pool.shape, lambda i, c, t, p: (0, 0, 0)),
                anywhere,
                anywhere,
                anywhere,
            ],
            out_specs=pl.BlockSpec((None, rows, cols), lambda i, c, t, p: (t[i], 0, 0)),
            scratch_shapes=[
                pltpu.VMEM((X, rows, depth), own.dtype),
                pltpu.VMEM((BLK, cols), jnp.float32),
                pltpu.SemaphoreType.DMA((X,)),
            ],
        ),
        out_shape=jax.ShapeDtypeStruct((X, rows, cols), dtype),
        compiler_params=params(),
        cost_estimate=pl.CostEstimate(
            flops=2 * rows * cols * depth, bytes_accessed=9 << 20, transcendentals=0
        ),
        name="alpha_partials",
    )(core, target, place, pool, own, near, far)


def alpha_kernel_entry(op, slots, block, core, target, place, *refs):
    alpha_kernel(op, slots, block, core, place, *refs)


def on_device(coeffs, a_blocks, a_list, a_count, b_blocks, b_list, b_count):
    operators, local_rows, slots, _ = a_blocks.shape
    local_cols = coeffs.shape[1]
    row_blocks = local_rows // BLK
    col_blocks = local_cols // BLK
    alpha_here = lax.axis_index("alpha")
    beta_here = lax.axis_index("beta")
    x_here = alpha_here // Z
    z_here = alpha_here % Z
    core_here = beta_here % CORES
    slot_ids = jnp.arange(slots, dtype=jnp.int32)

    local = b_list.reshape(operators, NBETA, col_blocks * slots) - beta_here * col_blocks
    inside = (local >= 0) & (local < col_blocks)
    lowest = jnp.min(jnp.where(inside, local, col_blocks - 1), axis=(0, 2))
    highest = jnp.max(jnp.where(inside, local, 0), axis=(0, 2))
    wanted = jnp.stack([lowest, highest], axis=1).reshape(NBETA * FROM_B)

    mine = lax.dynamic_slice_in_dim(b_list, beta_here * col_blocks, col_blocks, 1)
    owner = mine // col_blocks
    local_id = mine % col_blocks
    is_owner = owner[..., None] == jnp.arange(NBETA, dtype=jnp.int32)
    first = jnp.min(jnp.where(is_owner, local_id[..., None], col_blocks - 1), axis=(0, 1, 2))
    first_here = jnp.sum(jnp.where(is_owner, first, 0), axis=-1)
    beta_place = owner * FROM_B + (local_id != first_here).astype(jnp.int32)

    order = (x_here - jnp.arange(X, dtype=jnp.int32)) % X
    lists = a_list.reshape(operators, X, Z, row_blocks, slots)
    lists = lax.dynamic_index_in_dim(lists, z_here, 2, keepdims=False)
    counts = a_count.reshape(operators, X, Z, row_blocks)
    counts = lax.dynamic_index_in_dim(counts, z_here, 2, keepdims=False)
    per_x = Z * row_blocks
    here = (slot_ids < counts[..., None]) & (lists // per_x == x_here)
    by_x = jnp.where(here, lists % per_x, -1)
    pick = order[:, None] == jnp.arange(X, dtype=jnp.int32)
    alpha_place = jnp.sum(
        jnp.where(pick[None, :, :, None, None], by_x[:, None], 0), axis=2
    )

    a_flat = a_blocks.reshape(operators, local_rows, slots * BLK)
    a_half = lax.dynamic_index_in_dim(a_flat, core_here, 0, keepdims=False)
    near = [lax.ppermute(a_half, "alpha", shift_x(d)) for d in range(1, X)]
    near = jnp.stack(near)
    far = lax.ppermute(near, "beta", SWAP_CORES)
    beta_counts = lax.dynamic_slice_in_dim(b_count, beta_here * col_blocks, col_blocks, 1)
    beta_valid = slot_ids < beta_counts[..., None]
    b_flat = jnp.where(
        beta_valid[:, :, None, :, None],
        b_blocks.reshape(operators, col_blocks, BLK, slots, BLK),
        jnp.zeros((), b_blocks.dtype),
    ).reshape(operators, local_cols, slots * BLK)

    core = core_here.reshape(1)

    sent = pack(wanted, coeffs)
    pool_c = lax.all_to_all(sent, "beta", split_axis=0, concat_axis=0, tiled=True)
    d_one = beta_product(1, beta_place, pool_c, b_flat, None, jnp.bfloat16)

    c_along_z = lax.all_gather(coeffs, "alpha", axis=0, tiled=True, axis_index_groups=Z_GROUPS)
    inter_parts = alpha_partials(
        0, core, order, alpha_place, c_along_z, a_flat, near, far, jnp.bfloat16
    )
    inter_parts = lax.all_to_all(
        inter_parts, "alpha", split_axis=0, concat_axis=0, tiled=True, axis_index_groups=X_GROUPS
    )
    sent = sum_pack(wanted, inter_parts)
    pool_inter = lax.all_to_all(sent, "beta", split_axis=0, concat_axis=0, tiled=True)

    d_along_z = lax.all_gather(d_one, "alpha", axis=0, tiled=True, axis_index_groups=Z_GROUPS)
    sigma_parts = alpha_partials(
        1, core, order, alpha_place, d_along_z, a_flat, near, far, jnp.float32
    )
    sigma_one = lax.psum_scatter(
        sigma_parts.reshape(X * local_rows, local_cols),
        "alpha",
        scatter_dimension=0,
        tiled=True,
        axis_index_groups=X_GROUPS,
    )
    return beta_product(0, beta_place, pool_inter, b_flat, sigma_one, jnp.float32)


def solution(mesh):
    in_specs = (
        P("alpha", "beta"),
        P(None, "alpha", None, None),
        P(),
        P(),
        P(None, "beta", None, None),
        P(),
        P(),
    )
    return jax.shard_map(
        on_device, mesh=mesh, in_specs=in_specs, out_specs=P("alpha", "beta"), check_vma=False
    )
```

```python
import functools

import jax
import jax.numpy as jnp
from jax import lax
from jax.experimental import pallas as pl
from jax.experimental.pallas import tpu as pltpu
from jax.sharding import PartitionSpec as P

X, Z = 4, 8
Y, CORES = 8, 2
NBETA = Y * CORES
BLK = 128
FROM_B = 2
VMEM_LIMIT = 52 * 1024 * 1024

Z_GROUPS = [[x * Z + z for z in range(Z)] for x in range(X)]
X_GROUPS = [[x * Z + z for x in range(X)] for z in range(Z)]


def shift_x(step):
    return [(x * Z + z, (x + step) % X * Z + z) for x in range(X) for z in range(Z)]


SWAP_CORES = [(y * CORES + c, y * CORES + 1 - c) for y in range(Y) for c in range(CORES)]


def params():
    return pltpu.CompilerParams(vmem_limit_bytes=VMEM_LIMIT)


def pack_kernel(wanted, c_ref, out_ref, blocks, sems):
    for b in range(blocks.shape[0]):
        blocks[b] = c_ref[:, b * BLK : (b + 1) * BLK]

    def each(action):
        for t in range(NBETA * FROM_B):
            action(pltpu.make_async_copy(blocks.at[wanted[t]], out_ref.at[t], sems.at[t]))

    each(lambda copy: copy.start())
    each(lambda copy: copy.wait())


def pack(wanted, c):
    rows, cols = c.shape
    total = NBETA * FROM_B
    return pl.pallas_call(
        pack_kernel,
        grid_spec=pltpu.PrefetchScalarGridSpec(
            num_scalar_prefetch=1,
            grid=(1,),
            in_specs=[pl.BlockSpec(c.shape, lambda i, w: (0, 0))],
            out_specs=pl.BlockSpec(memory_space=pl.ANY),
            scratch_shapes=[
                pltpu.VMEM((cols // BLK, rows, BLK), c.dtype),
                pltpu.SemaphoreType.DMA((total,)),
            ],
        ),
        out_shape=jax.ShapeDtypeStruct((total, rows, BLK), c.dtype),
        compiler_params=params(),
        cost_estimate=pl.CostEstimate(flops=0, bytes_accessed=5 << 20, transcendentals=0),
        name="pack",
    )(wanted, c)


def sum_pack_kernel(wanted, *refs):
    parts, (out_ref, inter, sems) = refs[:X], refs[X:]
    step = pl.program_id(0)
    per_step = parts[0].shape[1] // BLK
    for b in range(per_step):
        columns = slice(b * BLK, (b + 1) * BLK)
        total = parts[0][:, columns]
        for part in parts[1:]:
            total += part[:, columns].astype(jnp.float32)
        inter[step * per_step + b] = total.astype(inter.dtype)

    def each(action):
        for t in range(NBETA * FROM_B):
            action(pltpu.make_async_copy(inter.at[wanted[t]], out_ref.at[t], sems.at[t]))

    @pl.when(step == pl.num_programs(0) - 1)
    def _():
        each(lambda copy: copy.start())
        each(lambda copy: copy.wait())


def sum_pack(wanted, parts, steps=2):
    rows, cols = parts[0].shape
    total = NBETA * FROM_B
    return pl.pallas_call(
        sum_pack_kernel,
        grid_spec=pltpu.PrefetchScalarGridSpec(
            num_scalar_prefetch=1,
            grid=(steps,),
            in_specs=[pl.BlockSpec((rows, cols // steps), lambda i, w: (0, i))] * X,
            out_specs=pl.BlockSpec(memory_space=pl.ANY),
            scratch_shapes=[
                pltpu.VMEM((cols // BLK, rows, BLK), jnp.bfloat16),
                pltpu.SemaphoreType.DMA((total,)),
            ],
        ),
        out_shape=jax.ShapeDtypeStruct((total, rows, BLK), jnp.bfloat16),
        compiler_params=params(),
        cost_estimate=pl.CostEstimate(flops=1 << 20, bytes_accessed=6 << 20, transcendentals=0),
        name="sum_pack",
    )(wanted, *parts)


def beta_kernel(op, place, count, pool_any, b_any, *rest):
    n = len(rest) // 2 - 2
    added_any, out_any, pool_ref, b_ref, added, out_ref, sems = (
        rest[:n],
        rest[n],
        rest[n + 1],
        rest[n + 2],
        rest[n + 3 : 2 * n + 3],
        rest[2 * n + 3],
        rest[2 * n + 4],
    )
    slots, cols, _ = b_ref.shape
    parts = 4
    width = cols // parts

    def factor_copy(i):
        span = pl.ds(i * width, width)
        return pltpu.make_async_copy(
            b_any.at[op, :, span, :], b_ref.at[:, span, :], sems.at[i]
        )

    def out_copy(i):
        span = pl.ds(i * width, width)
        return pltpu.make_async_copy(
            out_ref.at[:, span], out_any.at[:, span], sems.at[parts + i]
        )

    pool_copy = pltpu.make_async_copy(pool_any, pool_ref, sems.at[2 * parts])
    added_copies = [
        pltpu.make_async_copy(added_any[i], added[i], sems.at[2 * parts + 1 + i])
        for i in range(n)
    ]
    pool_copy.start()
    factor_copy(0).start()
    for copy in added_copies:
        copy.start()
    for i in range(1, parts):
        factor_copy(i).start()
    pool_copy.wait()
    for i in range(parts):
        factor_copy(i).wait()
        if i == 0:
            for copy in added_copies:
                copy.wait()
        for block in range(i * width // BLK, (i + 1) * width // BLK):
            columns = slice(block * BLK, (block + 1) * BLK)
            valid = count[op, block]
            picked = [pool_ref[place[op, block, s]] for s in range(slots)]
            factor = [
                jnp.where(s < valid, b_ref[s, columns], jnp.zeros((), b_ref.dtype))
                for s in range(slots)
            ]
            total = lax.dot_general(
                jnp.concatenate(picked, axis=1),
                jnp.concatenate(factor, axis=1),
                (((1,), (1,)), ((), ())),
                preferred_element_type=jnp.float32,
            )
            for part in added:
                total += part[:, columns].astype(jnp.float32)
            out_ref[:, columns] = total.astype(out_ref.dtype)
        out_copy(i).start()
    for i in range(parts):
        out_copy(i).wait()


def beta_product(op, place, count, pool, b_slots, added, dtype):
    _, slots, cols, _ = b_slots.shape
    rows = pool.shape[1]
    anywhere = pl.BlockSpec(memory_space=pl.ANY)
    return pl.pallas_call(
        functools.partial(beta_kernel, op),
        grid_spec=pltpu.PrefetchScalarGridSpec(
            num_scalar_prefetch=2,
            grid=(1,),
            in_specs=[
                anywhere,
                pl.BlockSpec(memory_space=pltpu.HBM),
                *([anywhere] * len(added)),
            ],
            out_specs=anywhere,
            scratch_shapes=[
                pltpu.VMEM(pool.shape, pool.dtype),
                pltpu.VMEM((slots, cols, BLK), b_slots.dtype),
                *[pltpu.VMEM(part.shape, part.dtype) for part in added],
                pltpu.VMEM((rows, cols), dtype),
                pltpu.SemaphoreType.DMA((9 + len(added),)),
            ],
        ),
        out_shape=jax.ShapeDtypeStruct((rows, cols), dtype),
        compiler_params=params(),
        cost_estimate=pl.CostEstimate(
            flops=2 * rows * cols * slots * BLK, bytes_accessed=7 << 20, transcendentals=0
        ),
        name="beta_product",
    )(place, count, pool, b_slots, *added)


FEW = 6
POOL_COPIES = 4


def alpha_kernel(op, core, lists, sizes, pool_any, own, *rest):
    near, far = rest[: X - 1], rest[X - 1 : 2 * (X - 1)]
    outs = rest[-X - 7 : -7]
    factors, pool_ref, own_out, sent_out, factor_sems, pool_sems, out_sems = rest[-7:]
    row_count, slots, _, _ = factors.shape
    blocks = row_count // X
    pool_blocks = pool_ref.shape[0]
    order = [*range(1, X), 0]

    def pool_copy(i):
        span = pl.ds(i * (pool_blocks // POOL_COPIES), pool_blocks // POOL_COPIES)
        return pltpu.make_async_copy(pool_any.at[span], pool_ref.at[span], pool_sems.at[i])

    def out_copy(t):
        source = sent_out.at[t - 1] if t else own_out
        return pltpu.make_async_copy(source, outs[t], out_sems.at[t])

    def fetch(source, t):
        for b in range(blocks):
            row = t * blocks + b

            def start(q, carry):
                pltpu.make_async_copy(
                    source.at[lists[op, row, q] // pool_blocks, pl.ds(b * BLK, BLK), :],
                    factors.at[row, q],
                    factor_sems.at[row, q],
                ).start()
                return carry

            lax.fori_loop(0, sizes[op, row], start, 0)

    for i in range(POOL_COPIES):
        pool_copy(i).start()

    @pl.when(core[0] == op)
    def _():
        for t in range(1, X):
            fetch(near[t - 1], t)

    @pl.when(core[0] != op)
    def _():
        for t in range(1, X):
            fetch(far[t - 1], t)

    fetch(own.at[op], 0)
    largest = sizes[op, 0]
    for row in range(row_count):

        def arrive(q, carry):
            pltpu.make_async_copy(
                own.at[op, 0, pl.ds(0, BLK), :], factors.at[row, q], factor_sems.at[row, q]
            ).wait()
            return carry

        lax.fori_loop(0, sizes[op, row], arrive, 0)
        largest = jnp.maximum(largest, sizes[op, row])
    for i in range(POOL_COPIES):
        pool_copy(i).wait()

    def multiply(depth):
        for t in order:
            for b in range(blocks):
                row = t * blocks + b
                size = sizes[op, row]
                left = [
                    jnp.where(q < size, factors[row, q], jnp.zeros((), factors.dtype))
                    for q in range(depth)
                ]
                right = [pool_ref[lists[op, row, q] % pool_blocks] for q in range(depth)]
                total = jnp.dot(
                    jnp.concatenate(left, axis=1),
                    jnp.concatenate(right, axis=0),
                    preferred_element_type=jnp.float32,
                )
                rows = slice(b * BLK, (b + 1) * BLK)
                if t:
                    sent_out[t - 1, rows, :] = total.astype(sent_out.dtype)
                else:
                    own_out[rows, :] = total
            out_copy(t).start()

    @pl.when(largest <= FEW)
    def _():
        multiply(FEW)

    @pl.when(largest > FEW)
    def _():
        multiply(slots)

    for t in order:
        out_copy(t).wait()


def alpha_partials(op, core, lists, sizes, gathered, own, near, far, after=()):
    _, slots, rows, _ = own.shape
    cols = gathered.shape[1]
    pool = gathered.reshape(gathered.shape[0] // BLK, BLK, cols)
    operands = [own, *near, *far, *after]
    row_count = X * rows // BLK
    anywhere = pl.BlockSpec(memory_space=pl.ANY)
    return pl.pallas_call(
        functools.partial(alpha_kernel, op),
        grid_spec=pltpu.PrefetchScalarGridSpec(
            num_scalar_prefetch=3,
            grid=(1,),
            in_specs=[
                pl.BlockSpec(memory_space=pltpu.HBM),
                *([anywhere] * len(operands)),
            ],
            out_specs=[anywhere] * X,
            scratch_shapes=[
                pltpu.VMEM((row_count, slots, BLK, BLK), own.dtype),
                pltpu.VMEM(pool.shape, pool.dtype),
                pltpu.VMEM((rows, cols), jnp.float32),
                pltpu.VMEM((X - 1, rows, cols), jnp.bfloat16),
                pltpu.SemaphoreType.DMA((row_count, slots)),
                pltpu.SemaphoreType.DMA((POOL_COPIES,)),
                pltpu.SemaphoreType.DMA((X,)),
            ],
        ),
        out_shape=[
            jax.ShapeDtypeStruct((rows, cols), jnp.bfloat16 if t else jnp.float32)
            for t in range(X)
        ],
        compiler_params=params(),
        cost_estimate=pl.CostEstimate(
            flops=2 * rows * cols * slots * BLK, bytes_accessed=9 << 20, transcendentals=0
        ),
        name="alpha_partials",
    )(core, lists, sizes, pool, *operands)


def to_their_rows(parts):
    sent = [lax.ppermute(parts[d], "alpha", shift_x(X - d)) for d in range(1, X)]
    return [parts[0], *sent]


def on_device(coeffs, a_blocks, a_list, a_count, b_blocks, b_list, b_count):
    operators, local_rows, slots, _ = a_blocks.shape
    local_cols = coeffs.shape[1]
    row_blocks = local_rows // BLK
    col_blocks = local_cols // BLK
    alpha_here = lax.axis_index("alpha")
    beta_here = lax.axis_index("beta")
    x_here = alpha_here // Z
    z_here = alpha_here % Z
    core_here = beta_here % CORES
    slot_ids = jnp.arange(slots, dtype=jnp.int32)

    local = b_list.reshape(operators, NBETA, col_blocks * slots) - beta_here * col_blocks
    inside = (local >= 0) & (local < col_blocks)
    lowest = jnp.min(jnp.where(inside, local, col_blocks - 1), axis=(0, 2))
    highest = jnp.max(jnp.where(inside, local, 0), axis=(0, 2))
    wanted = jnp.stack([lowest, highest], axis=1).reshape(NBETA * FROM_B)

    mine = lax.dynamic_slice_in_dim(b_list, beta_here * col_blocks, col_blocks, 1)
    beta_counts = lax.dynamic_slice_in_dim(b_count, beta_here * col_blocks, col_blocks, 1)
    owner = mine // col_blocks
    local_id = mine % col_blocks
    is_owner = owner[..., None] == jnp.arange(NBETA, dtype=jnp.int32)
    first = jnp.min(jnp.where(is_owner, local_id[..., None], col_blocks - 1), axis=(0, 1, 2))
    first_here = jnp.sum(jnp.where(is_owner, first, 0), axis=-1)
    beta_place = owner * FROM_B + (local_id != first_here).astype(jnp.int32)

    order = (x_here - jnp.arange(X, dtype=jnp.int32)) % X
    lists = a_list.reshape(operators, X, Z, row_blocks, slots)
    lists = lax.dynamic_index_in_dim(lists, z_here, 2, keepdims=False)
    counts = a_count.reshape(operators, X, Z, row_blocks)
    counts = lax.dynamic_index_in_dim(counts, z_here, 2, keepdims=False)
    per_x = Z * row_blocks
    here = (slot_ids < counts[..., None]) & (lists // per_x == x_here)
    code = slot_ids * per_x + lists % per_x
    earlier = slot_ids[:, None] > slot_ids
    rank = jnp.sum((here[..., None, :] & earlier).astype(jnp.int32), axis=-1)
    at_rank = here[..., None, :] & (rank[..., None, :] == slot_ids[:, None])
    lists = jnp.sum(jnp.where(at_rank, code[..., None, :], 0), axis=-1)
    sizes = jnp.sum(here.astype(jnp.int32), axis=-1)
    pick = order[:, None] == jnp.arange(X, dtype=jnp.int32)
    lists = jnp.sum(jnp.where(pick[None, :, :, None, None], lists[:, None], 0), axis=2)
    sizes = jnp.sum(jnp.where(pick[None, :, :, None], sizes[:, None], 0), axis=2)
    lists = lists.reshape(operators, X * row_blocks, slots)
    sizes = sizes.reshape(operators, X * row_blocks)

    a_slots = a_blocks.transpose(0, 2, 1, 3)
    b_slots = b_blocks.transpose(0, 2, 1, 3)
    a_half = lax.dynamic_index_in_dim(a_slots, core_here, 0, keepdims=False)
    near = [lax.ppermute(a_half, "alpha", shift_x(d)) for d in (1, 2)]
    a_half, beta_place, beta_counts, lists, sizes = lax.optimization_barrier(
        (a_half, beta_place, beta_counts, lists, sizes)
    )
    near.append(lax.ppermute(a_half, "alpha", shift_x(3)))
    far = [lax.ppermute(part, "beta", SWAP_CORES) for part in near]
    core = core_here.reshape(1)

    c_along_z = lax.all_gather(coeffs, "alpha", axis=0, tiled=True, axis_index_groups=Z_GROUPS)
    sent = pack(wanted, coeffs)
    pool_c = lax.all_to_all(sent, "beta", split_axis=0, concat_axis=0, tiled=True)
    d_one = beta_product(1, beta_place, beta_counts, pool_c, b_slots, (), jnp.bfloat16)
    c_along_z, d_one, near, far = lax.optimization_barrier((c_along_z, d_one, near, far))

    inter_parts = alpha_partials(0, core, lists, sizes, c_along_z, a_slots, near, far)
    sent = sum_pack(wanted, to_their_rows(inter_parts))
    pool_inter = lax.all_to_all(sent, "beta", split_axis=0, concat_axis=0, tiled=True)

    d_along_z = lax.all_gather(d_one, "alpha", axis=0, tiled=True, axis_index_groups=Z_GROUPS)
    sigma_parts = alpha_partials(
        1, core, lists, sizes, d_along_z, a_slots, near, far, after=(sent,)
    )
    sigma_one = to_their_rows(sigma_parts)
    return beta_product(0, beta_place, beta_counts, pool_inter, b_slots, sigma_one, jnp.float32)


def solution(mesh):
    in_specs = (
        P("alpha", "beta"),
        P(None, "alpha", None, None),
        P(),
        P(),
        P(None, "beta", None, None),
        P(),
        P(),
    )
    return jax.shard_map(
        on_device, mesh=mesh, in_specs=in_specs, out_specs=P("alpha", "beta"), check_vma=False
    )
```

```python
import functools

import jax
import jax.numpy as jnp
from jax import lax
from jax.experimental import pallas as pl
from jax.experimental.pallas import tpu as pltpu
from jax.sharding import PartitionSpec as P

X, Z = 4, 8
Y, CORES = 8, 2
NBETA = Y * CORES
BLK = 128
FROM_B = 2
VMEM_LIMIT = 50 * 1024 * 1024

Z_GROUPS = [[x * Z + z for z in range(Z)] for x in range(X)]
X_GROUPS = [[x * Z + z for x in range(X)] for z in range(Z)]


def shift_x(step):
    return [(x * Z + z, (x + step) % X * Z + z) for x in range(X) for z in range(Z)]


SWAP_CORES = [(y * CORES + c, y * CORES + 1 - c) for y in range(Y) for c in range(CORES)]


def params():
    return pltpu.CompilerParams(vmem_limit_bytes=VMEM_LIMIT)


def pack_kernel(wanted, c_ref, out_ref, blocks, sems):
    for b in range(blocks.shape[0]):
        blocks[b] = c_ref[:, b * BLK : (b + 1) * BLK]

    def each(action):
        for t in range(NBETA * FROM_B):
            action(pltpu.make_async_copy(blocks.at[wanted[t]], out_ref.at[t], sems.at[t]))

    each(lambda copy: copy.start())
    each(lambda copy: copy.wait())


def pack(wanted, c):
    rows, cols = c.shape
    total = NBETA * FROM_B
    return pl.pallas_call(
        pack_kernel,
        grid_spec=pltpu.PrefetchScalarGridSpec(
            num_scalar_prefetch=1,
            grid=(1,),
            in_specs=[pl.BlockSpec(c.shape, lambda i, w: (0, 0))],
            out_specs=pl.BlockSpec(memory_space=pl.ANY),
            scratch_shapes=[
                pltpu.VMEM((cols // BLK, rows, BLK), c.dtype),
                pltpu.SemaphoreType.DMA((total,)),
            ],
        ),
        out_shape=jax.ShapeDtypeStruct((total, rows, BLK), c.dtype),
        compiler_params=params(),
        cost_estimate=pl.CostEstimate(flops=0, bytes_accessed=5 << 20, transcendentals=0),
        name="pack",
    )(wanted, c)


def sum_pack_kernel(wanted, *refs):
    parts, (out_ref, inter, sems) = refs[:-3], refs[-3:]
    step = pl.program_id(0)
    per_step = parts[0].shape[1] // BLK
    for b in range(per_step):
        columns = slice(b * BLK, (b + 1) * BLK)
        total = parts[0][:, columns]
        for part in parts[1:]:
            total += part[:, columns].astype(jnp.float32)
        inter[step * per_step + b] = total.astype(inter.dtype)

    def each(action):
        for t in range(NBETA * FROM_B):
            action(pltpu.make_async_copy(inter.at[wanted[t]], out_ref.at[t], sems.at[t]))

    @pl.when(step == pl.num_programs(0) - 1)
    def _():
        each(lambda copy: copy.start())
        each(lambda copy: copy.wait())


def sum_pack(wanted, parts, steps=2):
    rows, cols = parts[0].shape
    total = NBETA * FROM_B
    return pl.pallas_call(
        sum_pack_kernel,
        grid_spec=pltpu.PrefetchScalarGridSpec(
            num_scalar_prefetch=1,
            grid=(steps,),
            in_specs=[pl.BlockSpec((rows, cols // steps), lambda i, w: (0, i))] * len(parts),
            out_specs=pl.BlockSpec(memory_space=pl.ANY),
            scratch_shapes=[
                pltpu.VMEM((cols // BLK, rows, BLK), jnp.bfloat16),
                pltpu.SemaphoreType.DMA((total,)),
            ],
        ),
        out_shape=jax.ShapeDtypeStruct((total, rows, BLK), jnp.bfloat16),
        compiler_params=params(),
        cost_estimate=pl.CostEstimate(flops=1 << 20, bytes_accessed=6 << 20, transcendentals=0),
        name="sum_pack",
    )(wanted, *parts)


def beta_kernel(op, place, count, pool_any, b_any, *rest):
    n = len(rest) // 2 - 2
    added_any, out_any, pool_ref, b_ref, added, out_ref, sems = (
        rest[:n],
        rest[n],
        rest[n + 1],
        rest[n + 2],
        rest[n + 3 : 2 * n + 3],
        rest[2 * n + 3],
        rest[2 * n + 4],
    )
    slots, cols, _ = b_ref.shape
    parts = 4
    width = cols // parts

    def factor_copy(i):
        span = pl.ds(i * width, width)
        return pltpu.make_async_copy(
            b_any.at[op, :, span, :], b_ref.at[:, span, :], sems.at[i]
        )

    def out_copy(i):
        span = pl.ds(i * width, width)
        return pltpu.make_async_copy(
            out_ref.at[:, span], out_any.at[:, span], sems.at[parts + i]
        )

    pool_copy = pltpu.make_async_copy(pool_any, pool_ref, sems.at[2 * parts])
    added_copies = [
        pltpu.make_async_copy(added_any[i], added[i], sems.at[2 * parts + 1 + i])
        for i in range(n)
    ]
    pool_copy.start()
    factor_copy(0).start()
    for copy in added_copies:
        copy.start()
    for i in range(1, parts):
        factor_copy(i).start()
    pool_copy.wait()
    for i in range(parts):
        factor_copy(i).wait()
        if i == 0:
            for copy in added_copies:
                copy.wait()
        for block in range(i * width // BLK, (i + 1) * width // BLK):
            columns = slice(block * BLK, (block + 1) * BLK)
            valid = count[op, block]
            picked = [pool_ref[place[op, block, s]] for s in range(slots)]
            factor = [
                jnp.where(s < valid, b_ref[s, columns], jnp.zeros((), b_ref.dtype))
                for s in range(slots)
            ]
            total = lax.dot_general(
                jnp.concatenate(picked, axis=1),
                jnp.concatenate(factor, axis=1),
                (((1,), (1,)), ((), ())),
                preferred_element_type=jnp.float32,
            )
            for part in added:
                total += part[:, columns].astype(jnp.float32)
            out_ref[:, columns] = total.astype(out_ref.dtype)
        out_copy(i).start()
    for i in range(parts):
        out_copy(i).wait()


def beta_product(op, place, count, pool, b_slots, added, dtype):
    _, slots, cols, _ = b_slots.shape
    rows = pool.shape[1]
    anywhere = pl.BlockSpec(memory_space=pl.ANY)
    return pl.pallas_call(
        functools.partial(beta_kernel, op),
        grid_spec=pltpu.PrefetchScalarGridSpec(
            num_scalar_prefetch=2,
            grid=(1,),
            in_specs=[
                anywhere,
                pl.BlockSpec(memory_space=pltpu.HBM),
                *([anywhere] * len(added)),
            ],
            out_specs=anywhere,
            scratch_shapes=[
                pltpu.VMEM(pool.shape, pool.dtype),
                pltpu.VMEM((slots, cols, BLK), b_slots.dtype),
                *[pltpu.VMEM(part.shape, part.dtype) for part in added],
                pltpu.VMEM((rows, cols), dtype),
                pltpu.SemaphoreType.DMA((9 + len(added),)),
            ],
        ),
        out_shape=jax.ShapeDtypeStruct((rows, cols), dtype),
        compiler_params=params(),
        cost_estimate=pl.CostEstimate(
            flops=2 * rows * cols * slots * BLK, bytes_accessed=7 << 20, transcendentals=0
        ),
        name="beta_product",
    )(place, count, pool, b_slots, *added)


FEW = 6
POOL_COPIES = 4


def alpha_kernel(op, steps, core, lists, sizes, pool_any, own, *rest):
    near, far = rest[: X - 1], rest[X - 1 : 2 * (X - 1)]
    outs = rest[-len(steps) - 6 : -6]
    factors, pool_ref, results, factor_sems, pool_sems, out_sems = rest[-6:]
    row_count, slots, _, _ = factors.shape
    blocks = row_count // len(steps)
    pool_blocks = pool_ref.shape[0]

    def pool_copy(i):
        span = pl.ds(i * (pool_blocks // POOL_COPIES), pool_blocks // POOL_COPIES)
        return pltpu.make_async_copy(pool_any.at[span], pool_ref.at[span], pool_sems.at[i])

    def out_copy(i):
        return pltpu.make_async_copy(results[i], outs[i], out_sems.at[i])

    def fetch(source, i):
        for b in range(blocks):
            listed, row = steps[i] * blocks + b, i * blocks + b

            def start(q, carry):
                pltpu.make_async_copy(
                    source.at[lists[op, listed, q] // pool_blocks, pl.ds(b * BLK, BLK), :],
                    factors.at[row, q],
                    factor_sems.at[row, q],
                ).start()
                return carry

            lax.fori_loop(0, sizes[op, listed], start, 0)

    for i in range(POOL_COPIES):
        pool_copy(i).start()

    @pl.when(core[0] == op)
    def _():
        for i, t in enumerate(steps):
            if t:
                fetch(near[t - 1], i)

    @pl.when(core[0] != op)
    def _():
        for i, t in enumerate(steps):
            if t:
                fetch(far[t - 1], i)

    for i, t in enumerate(steps):
        if not t:
            fetch(own.at[op], i)
    largest = jnp.int32(0)
    for row in range(row_count):
        listed = steps[row // blocks] * blocks + row % blocks

        def arrive(q, carry):
            pltpu.make_async_copy(
                own.at[op, 0, pl.ds(0, BLK), :], factors.at[row, q], factor_sems.at[row, q]
            ).wait()
            return carry

        lax.fori_loop(0, sizes[op, listed], arrive, 0)
        largest = jnp.maximum(largest, sizes[op, listed])
    for i in range(POOL_COPIES):
        pool_copy(i).wait()

    def multiply(depth):
        for i, t in enumerate(steps):
            for b in range(blocks):
                listed, row = t * blocks + b, i * blocks + b
                size = sizes[op, listed]
                left = [
                    jnp.where(q < size, factors[row, q], jnp.zeros((), factors.dtype))
                    for q in range(depth)
                ]
                right = [pool_ref[lists[op, listed, q] % pool_blocks] for q in range(depth)]
                total = jnp.dot(
                    jnp.concatenate(left, axis=1),
                    jnp.concatenate(right, axis=0),
                    preferred_element_type=jnp.float32,
                )
                results[i][b * BLK : (b + 1) * BLK, :] = total.astype(results[i].dtype)
            out_copy(i).start()

    @pl.when(largest <= FEW)
    def _():
        multiply(FEW)

    @pl.when(largest > FEW)
    def _():
        multiply(slots)

    for i in range(len(steps)):
        out_copy(i).wait()


def alpha_products(op, steps, core, lists, sizes, gathered, own, near, far, after):
    _, slots, rows, _ = own.shape
    cols = gathered.shape[1]
    pool = gathered.reshape(gathered.shape[0] // BLK, BLK, cols)
    operands = [own, *near, *far, *after]
    row_count = len(steps) * rows // BLK
    anywhere = pl.BlockSpec(memory_space=pl.ANY)
    types = [jnp.bfloat16 if t else jnp.float32 for t in steps]
    return pl.pallas_call(
        functools.partial(alpha_kernel, op, steps),
        grid_spec=pltpu.PrefetchScalarGridSpec(
            num_scalar_prefetch=3,
            grid=(1,),
            in_specs=[anywhere] * (1 + len(operands)),
            out_specs=[anywhere] * len(steps),
            scratch_shapes=[
                pltpu.VMEM((row_count, slots, BLK, BLK), own.dtype),
                pltpu.VMEM(pool.shape, pool.dtype),
                [pltpu.VMEM((rows, cols), kind) for kind in types],
                pltpu.SemaphoreType.DMA((row_count, slots)),
                pltpu.SemaphoreType.DMA((POOL_COPIES,)),
                pltpu.SemaphoreType.DMA((len(steps),)),
            ],
        ),
        out_shape=[jax.ShapeDtypeStruct((rows, cols), kind) for kind in types],
        compiler_params=params(),
        cost_estimate=pl.CostEstimate(
            flops=rows * cols * slots * BLK, bytes_accessed=12 << 20, transcendentals=0
        ),
        name="alpha_products",
    )(core, lists, sizes, pool, *operands)


def alpha_sums(op, core, lists, sizes, gathered, own, near, far, after=()):
    common = (core, lists, sizes, gathered, own, near, far)
    (across,) = alpha_products(op, (2,), *common, after)
    after_one, before_one, here = alpha_products(op, (1, 3, 0), *common, (across,))
    from_across = lax.ppermute(across, "alpha", shift_x(X - 2))
    sent = [
        lax.ppermute(part, "alpha", shift_x(X - d)) for d, part in ((1, after_one), (3, before_one))
    ]
    return [fold(here, from_across), *sent]


def fold_kernel(here_ref, other_ref, out_ref):
    out_ref[...] = here_ref[...] + other_ref[...].astype(jnp.float32)


def fold(here, other):
    rows, cols = here.shape
    by_rows = pl.BlockSpec((rows // 2, cols), lambda i: (i, 0))
    return pl.pallas_call(
        fold_kernel,
        grid=(2,),
        in_specs=[by_rows] * 2,
        out_specs=by_rows,
        out_shape=jax.ShapeDtypeStruct(here.shape, jnp.float32),
        compiler_params=params(),
        cost_estimate=pl.CostEstimate(flops=1 << 20, bytes_accessed=48 << 20, transcendentals=0),
        name="fold",
    )(here, other)


def on_device(coeffs, a_blocks, a_list, a_count, b_blocks, b_list, b_count):
    operators, local_rows, slots, _ = a_blocks.shape
    local_cols = coeffs.shape[1]
    row_blocks = local_rows // BLK
    col_blocks = local_cols // BLK
    alpha_here = lax.axis_index("alpha")
    beta_here = lax.axis_index("beta")
    x_here = alpha_here // Z
    z_here = alpha_here % Z
    core_here = beta_here % CORES
    slot_ids = jnp.arange(slots, dtype=jnp.int32)

    local = b_list.reshape(operators, NBETA, col_blocks * slots) - beta_here * col_blocks
    inside = (local >= 0) & (local < col_blocks)
    lowest = jnp.min(jnp.where(inside, local, col_blocks - 1), axis=(0, 2))
    highest = jnp.max(jnp.where(inside, local, 0), axis=(0, 2))
    wanted = jnp.stack([lowest, highest], axis=1).reshape(NBETA * FROM_B)

    mine = lax.dynamic_slice_in_dim(b_list, beta_here * col_blocks, col_blocks, 1)
    beta_counts = lax.dynamic_slice_in_dim(b_count, beta_here * col_blocks, col_blocks, 1)
    owner = mine // col_blocks
    local_id = mine % col_blocks
    is_owner = owner[..., None] == jnp.arange(NBETA, dtype=jnp.int32)
    first = jnp.min(jnp.where(is_owner, local_id[..., None], col_blocks - 1), axis=(0, 1, 2))
    first_here = jnp.sum(jnp.where(is_owner, first, 0), axis=-1)
    beta_place = owner * FROM_B + (local_id != first_here).astype(jnp.int32)

    order = (x_here - jnp.arange(X, dtype=jnp.int32)) % X
    lists = a_list.reshape(operators, X, Z, row_blocks, slots)
    lists = lax.dynamic_index_in_dim(lists, z_here, 2, keepdims=False)
    counts = a_count.reshape(operators, X, Z, row_blocks)
    counts = lax.dynamic_index_in_dim(counts, z_here, 2, keepdims=False)
    per_x = Z * row_blocks
    here = (slot_ids < counts[..., None]) & (lists // per_x == x_here)
    code = slot_ids * per_x + lists % per_x
    earlier = slot_ids[:, None] > slot_ids
    rank = jnp.sum((here[..., None, :] & earlier).astype(jnp.int32), axis=-1)
    at_rank = here[..., None, :] & (rank[..., None, :] == slot_ids[:, None])
    lists = jnp.sum(jnp.where(at_rank, code[..., None, :], 0), axis=-1)
    sizes = jnp.sum(here.astype(jnp.int32), axis=-1)
    pick = order[:, None] == jnp.arange(X, dtype=jnp.int32)
    lists = jnp.sum(jnp.where(pick[None, :, :, None, None], lists[:, None], 0), axis=2)
    sizes = jnp.sum(jnp.where(pick[None, :, :, None], sizes[:, None], 0), axis=2)
    lists = lists.reshape(operators, X * row_blocks, slots)
    sizes = sizes.reshape(operators, X * row_blocks)

    a_slots = a_blocks.transpose(0, 2, 1, 3)
    b_slots = b_blocks.transpose(0, 2, 1, 3)
    a_half = lax.dynamic_index_in_dim(a_slots, core_here, 0, keepdims=False)
    near = [lax.ppermute(a_half, "alpha", shift_x(d)) for d in (1, 2)]
    a_half, beta_place, beta_counts, lists, sizes = lax.optimization_barrier(
        (a_half, beta_place, beta_counts, lists, sizes)
    )
    near.append(lax.ppermute(a_half, "alpha", shift_x(3)))
    far = [lax.ppermute(part, "beta", SWAP_CORES) for part in near]
    core = core_here.reshape(1)

    c_along_z = lax.all_gather(coeffs, "alpha", axis=0, tiled=True, axis_index_groups=Z_GROUPS)
    sent = pack(wanted, coeffs)
    pool_c = lax.all_to_all(sent, "beta", split_axis=0, concat_axis=0, tiled=True)
    d_one = beta_product(1, beta_place, beta_counts, pool_c, b_slots, (), jnp.bfloat16)
    c_along_z, d_one, near, far = lax.optimization_barrier((c_along_z, d_one, near, far))

    inter_parts = alpha_sums(0, core, lists, sizes, c_along_z, a_slots, near, far)
    sent = sum_pack(wanted, inter_parts)
    pool_inter = lax.all_to_all(sent, "beta", split_axis=0, concat_axis=0, tiled=True)

    d_along_z = lax.all_gather(d_one, "alpha", axis=0, tiled=True, axis_index_groups=Z_GROUPS)
    sigma_one = alpha_sums(
        1, core, lists, sizes, d_along_z, a_slots, near, far, after=(sent,)
    )
    return beta_product(0, beta_place, beta_counts, pool_inter, b_slots, sigma_one, jnp.float32)


def solution(mesh):
    in_specs = (
        P("alpha", "beta"),
        P(None, "alpha", None, None),
        P(),
        P(),
        P(None, "beta", None, None),
        P(),
        P(),
    )
    return jax.shard_map(
        on_device, mesh=mesh, in_specs=in_specs, out_specs=P("alpha", "beta"), check_vma=False
    )
```

```python
import functools

import jax
import jax.numpy as jnp
from jax import lax
from jax.experimental import pallas as pl
from jax.experimental.pallas import tpu as pltpu
from jax.sharding import PartitionSpec as P

X, Z = 4, 8
Y, CORES = 8, 2
NBETA = Y * CORES
BLK = 128
FROM_B = 2
VMEM_LIMIT = 50 * 1024 * 1024

Z_GROUPS = [[x * Z + z for z in range(Z)] for x in range(X)]
X_GROUPS = [[x * Z + z for x in range(X)] for z in range(Z)]


def shift_x(step):
    return [(x * Z + z, (x + step) % X * Z + z) for x in range(X) for z in range(Z)]


SWAP_CORES = [(y * CORES + c, y * CORES + 1 - c) for y in range(Y) for c in range(CORES)]


def params(limit=VMEM_LIMIT):
    return pltpu.CompilerParams(vmem_limit_bytes=limit)


def pack_kernel(wanted, c_ref, out_ref, blocks, sems):
    for b in range(blocks.shape[0]):
        blocks[b] = c_ref[:, b * BLK : (b + 1) * BLK]

    def each(action):
        for t in range(NBETA * FROM_B):
            action(pltpu.make_async_copy(blocks.at[wanted[t]], out_ref.at[t], sems.at[t]))

    each(lambda copy: copy.start())
    each(lambda copy: copy.wait())


def pack(wanted, c):
    rows, cols = c.shape
    total = NBETA * FROM_B
    return pl.pallas_call(
        pack_kernel,
        grid_spec=pltpu.PrefetchScalarGridSpec(
            num_scalar_prefetch=1,
            grid=(1,),
            in_specs=[pl.BlockSpec(c.shape, lambda i, w: (0, 0))],
            out_specs=pl.BlockSpec(memory_space=pl.ANY),
            scratch_shapes=[
                pltpu.VMEM((cols // BLK, rows, BLK), c.dtype),
                pltpu.SemaphoreType.DMA((total,)),
            ],
        ),
        out_shape=jax.ShapeDtypeStruct((total, rows, BLK), c.dtype),
        compiler_params=params(60 * 1024 * 1024),
        cost_estimate=pl.CostEstimate(flops=0, bytes_accessed=5 << 20, transcendentals=0),
        name="pack",
    )(wanted, c)


def sum_pack_kernel(wanted, *refs):
    parts, (out_ref, inter, sems) = refs[:-3], refs[-3:]
    step = pl.program_id(0)
    per_step = parts[0].shape[1] // BLK
    for b in range(per_step):
        columns = slice(b * BLK, (b + 1) * BLK)
        total = parts[0][:, columns]
        for part in parts[1:]:
            total += part[:, columns].astype(jnp.float32)
        inter[step * per_step + b] = total.astype(inter.dtype)

    def each(action):
        for t in range(NBETA * FROM_B):
            action(pltpu.make_async_copy(inter.at[wanted[t]], out_ref.at[t], sems.at[t]))

    @pl.when(step == pl.num_programs(0) - 1)
    def _():
        each(lambda copy: copy.start())
        each(lambda copy: copy.wait())


def sum_pack(wanted, parts, steps=2):
    rows, cols = parts[0].shape
    total = NBETA * FROM_B
    return pl.pallas_call(
        sum_pack_kernel,
        grid_spec=pltpu.PrefetchScalarGridSpec(
            num_scalar_prefetch=1,
            grid=(steps,),
            in_specs=[pl.BlockSpec((rows, cols // steps), lambda i, w: (0, i))] * len(parts),
            out_specs=pl.BlockSpec(memory_space=pl.ANY),
            scratch_shapes=[
                pltpu.VMEM((cols // BLK, rows, BLK), jnp.bfloat16),
                pltpu.SemaphoreType.DMA((total,)),
            ],
        ),
        out_shape=jax.ShapeDtypeStruct((total, rows, BLK), jnp.bfloat16),
        compiler_params=params(),
        cost_estimate=pl.CostEstimate(flops=1 << 20, bytes_accessed=6 << 20, transcendentals=0),
        name="sum_pack",
    )(wanted, *parts)


def beta_kernel(op, place, count, pool_any, b_any, *rest):
    n = len(rest) // 2 - 2
    added_any, out_any, pool_ref, b_ref, added, out_ref, sems = (
        rest[:n],
        rest[n],
        rest[n + 1],
        rest[n + 2],
        rest[n + 3 : 2 * n + 3],
        rest[2 * n + 3],
        rest[2 * n + 4],
    )
    slots, cols, _ = b_ref.shape
    parts = 4
    width = cols // parts

    def factor_copy(i):
        span = pl.ds(i * width, width)
        return pltpu.make_async_copy(
            b_any.at[op, :, span, :], b_ref.at[:, span, :], sems.at[i]
        )

    def out_copy(i):
        span = pl.ds(i * width, width)
        return pltpu.make_async_copy(
            out_ref.at[:, span], out_any.at[:, span], sems.at[parts + i]
        )

    pool_copy = pltpu.make_async_copy(pool_any, pool_ref, sems.at[2 * parts])
    added_copies = [
        pltpu.make_async_copy(added_any[i], added[i], sems.at[2 * parts + 1 + i])
        for i in range(n)
    ]
    pool_copy.start()
    factor_copy(0).start()
    for copy in added_copies:
        copy.start()
    for i in range(1, parts):
        factor_copy(i).start()
    pool_copy.wait()
    for i in range(parts):
        factor_copy(i).wait()
        if i == 0:
            for copy in added_copies:
                copy.wait()
        for block in range(i * width // BLK, (i + 1) * width // BLK):
            columns = slice(block * BLK, (block + 1) * BLK)
            valid = count[op, block]
            picked = [pool_ref[place[op, block, s]] for s in range(slots)]
            factor = [
                jnp.where(s < valid, b_ref[s, columns], jnp.zeros((), b_ref.dtype))
                for s in range(slots)
            ]
            total = lax.dot_general(
                jnp.concatenate(picked, axis=1),
                jnp.concatenate(factor, axis=1),
                (((1,), (1,)), ((), ())),
                preferred_element_type=jnp.float32,
            )
            for part in added:
                total += part[:, columns].astype(jnp.float32)
            out_ref[:, columns] = total.astype(out_ref.dtype)
        out_copy(i).start()
    for i in range(parts):
        out_copy(i).wait()


def beta_product(op, place, count, pool, b_slots, added, dtype):
    _, slots, cols, _ = b_slots.shape
    rows = pool.shape[1]
    anywhere = pl.BlockSpec(memory_space=pl.ANY)
    return pl.pallas_call(
        functools.partial(beta_kernel, op),
        grid_spec=pltpu.PrefetchScalarGridSpec(
            num_scalar_prefetch=2,
            grid=(1,),
            in_specs=[
                anywhere,
                pl.BlockSpec(memory_space=pltpu.HBM),
                *([anywhere] * len(added)),
            ],
            out_specs=anywhere,
            scratch_shapes=[
                pltpu.VMEM(pool.shape, pool.dtype),
                pltpu.VMEM((slots, cols, BLK), b_slots.dtype),
                *[pltpu.VMEM(part.shape, part.dtype) for part in added],
                pltpu.VMEM((rows, cols), dtype),
                pltpu.SemaphoreType.DMA((9 + len(added),)),
            ],
        ),
        out_shape=jax.ShapeDtypeStruct((rows, cols), dtype),
        compiler_params=params(),
        cost_estimate=pl.CostEstimate(
            flops=2 * rows * cols * slots * BLK, bytes_accessed=7 << 20, transcendentals=0
        ),
        name="beta_product",
    )(place, count, pool, b_slots, *added)


FEW = 6


def alpha_kernel(op, steps, core, lists, sizes, pool_any, own, *rest):
    near, far = rest[: X - 1], rest[X - 1 : 2 * (X - 1)]
    outs = rest[-len(steps) - 6 : -6]
    factors, listed_blocks, results, factor_sems, block_sems, out_sems = rest[-6:]
    row_count, slots, _, _ = factors.shape
    blocks = row_count // len(steps)
    pool_blocks = pool_any.shape[0]

    def out_copy(i):
        return pltpu.make_async_copy(results[i], outs[i], out_sems.at[i])

    def fetch(source, i):
        for b in range(blocks):
            listed, row = steps[i] * blocks + b, i * blocks + b

            def start(q, carry):
                code = lists[op, listed, q]
                pltpu.make_async_copy(
                    pool_any.at[code % pool_blocks],
                    listed_blocks.at[row, q],
                    block_sems.at[row, q],
                ).start()
                pltpu.make_async_copy(
                    source.at[code // pool_blocks, pl.ds(b * BLK, BLK), :],
                    factors.at[row, q],
                    factor_sems.at[row, q],
                ).start()
                return carry

            lax.fori_loop(0, sizes[op, listed], start, 0)

    @pl.when(core[0] == op)
    def _():
        for i, t in enumerate(steps):
            if t:
                fetch(near[t - 1], i)

    @pl.when(core[0] != op)
    def _():
        for i, t in enumerate(steps):
            if t:
                fetch(far[t - 1], i)

    for i, t in enumerate(steps):
        if not t:
            fetch(own.at[op], i)
    largest = jnp.int32(0)
    for row in range(row_count):
        listed = steps[row // blocks] * blocks + row % blocks

        def arrive(q, carry):
            pltpu.make_async_copy(
                own.at[op, 0, pl.ds(0, BLK), :], factors.at[row, q], factor_sems.at[row, q]
            ).wait()
            pltpu.make_async_copy(
                pool_any.at[0], listed_blocks.at[row, q], block_sems.at[row, q]
            ).wait()
            return carry

        lax.fori_loop(0, sizes[op, listed], arrive, 0)
        largest = jnp.maximum(largest, sizes[op, listed])

    def multiply(depth):
        for i, t in enumerate(steps):
            for b in range(blocks):
                listed, row = t * blocks + b, i * blocks + b
                size = sizes[op, listed]
                left = [
                    jnp.where(q < size, factors[row, q], jnp.zeros((), factors.dtype))
                    for q in range(depth)
                ]
                right = [
                    jnp.where(
                        q < size, listed_blocks[row, q], jnp.zeros((), listed_blocks.dtype)
                    )
                    for q in range(depth)
                ]
                total = jnp.dot(
                    jnp.concatenate(left, axis=1),
                    jnp.concatenate(right, axis=0),
                    preferred_element_type=jnp.float32,
                )
                results[i][b * BLK : (b + 1) * BLK, :] = total.astype(results[i].dtype)
            out_copy(i).start()

    @pl.when(largest <= FEW)
    def _():
        multiply(FEW)

    @pl.when(largest > FEW)
    def _():
        multiply(slots)

    for i in range(len(steps)):
        out_copy(i).wait()


def alpha_products(op, steps, core, lists, sizes, gathered, own, near, far, after):
    _, slots, rows, _ = own.shape
    cols = gathered.shape[1]
    pool = gathered.reshape(gathered.shape[0] // BLK, BLK, cols)
    operands = [own, *near, *far, *after]
    row_count = len(steps) * rows // BLK
    anywhere = pl.BlockSpec(memory_space=pl.ANY)
    types = [jnp.bfloat16 if t else jnp.float32 for t in steps]
    return pl.pallas_call(
        functools.partial(alpha_kernel, op, steps),
        grid_spec=pltpu.PrefetchScalarGridSpec(
            num_scalar_prefetch=3,
            grid=(1,),
            in_specs=[anywhere] * (1 + len(operands)),
            out_specs=[anywhere] * len(steps),
            scratch_shapes=[
                pltpu.VMEM((row_count, slots, BLK, BLK), own.dtype),
                pltpu.VMEM((row_count, slots, BLK, cols), pool.dtype),
                [pltpu.VMEM((rows, cols), kind) for kind in types],
                pltpu.SemaphoreType.DMA((row_count, slots)),
                pltpu.SemaphoreType.DMA((row_count, slots)),
                pltpu.SemaphoreType.DMA((len(steps),)),
            ],
        ),
        out_shape=[jax.ShapeDtypeStruct((rows, cols), kind) for kind in types],
        compiler_params=params(),
        cost_estimate=pl.CostEstimate(
            flops=rows * cols * slots * BLK, bytes_accessed=12 << 20, transcendentals=0
        ),
        name="alpha_products",
    )(core, lists, sizes, pool, *operands)


def alpha_sums(op, core, lists, sizes, gathered, own, near, far, after=()):
    common = (core, lists, sizes, gathered, own, near, far)
    (across,) = alpha_products(op, (2,), *common, after)
    after_one, before_one = alpha_products(op, (1, 3), *common, (across,))
    (here,) = alpha_products(op, (0,), *common, (after_one,))
    from_across = lax.ppermute(across, "alpha", shift_x(X - 2))
    sent = [
        lax.ppermute(part, "alpha", shift_x(X - d)) for d, part in ((1, after_one), (3, before_one))
    ]
    return [fold(here, from_across), *sent]


def fold_kernel(first_ref, *refs):
    total = first_ref[...]
    for ref in refs[:-1]:
        total += ref[...].astype(jnp.float32)
    refs[-1][...] = total


def fold(first, *others):
    rows, cols = first.shape
    by_rows = pl.BlockSpec((rows // 2, cols), lambda i: (i, 0))
    return pl.pallas_call(
        fold_kernel,
        grid=(2,),
        in_specs=[by_rows] * (1 + len(others)),
        out_specs=by_rows,
        out_shape=jax.ShapeDtypeStruct(first.shape, jnp.float32),
        compiler_params=params(),
        cost_estimate=pl.CostEstimate(flops=1 << 20, bytes_accessed=48 << 20, transcendentals=0),
        name="fold",
    )(first, *others)


def on_device(coeffs, a_blocks, a_list, a_count, b_blocks, b_list, b_count):
    operators, local_rows, slots, _ = a_blocks.shape
    local_cols = coeffs.shape[1]
    row_blocks = local_rows // BLK
    col_blocks = local_cols // BLK
    alpha_here = lax.axis_index("alpha")
    beta_here = lax.axis_index("beta")
    x_here = alpha_here // Z
    z_here = alpha_here % Z
    core_here = beta_here % CORES
    slot_ids = jnp.arange(slots, dtype=jnp.int32)

    local = b_list.reshape(operators, NBETA, col_blocks * slots) - beta_here * col_blocks
    inside = (local >= 0) & (local < col_blocks)
    lowest = jnp.min(jnp.where(inside, local, col_blocks - 1), axis=(0, 2))
    highest = jnp.max(jnp.where(inside, local, 0), axis=(0, 2))
    wanted = jnp.stack([lowest, highest], axis=1).reshape(NBETA * FROM_B)

    mine = lax.dynamic_slice_in_dim(b_list, beta_here * col_blocks, col_blocks, 1)
    beta_counts = lax.dynamic_slice_in_dim(b_count, beta_here * col_blocks, col_blocks, 1)
    owner = mine // col_blocks
    local_id = mine % col_blocks
    is_owner = owner[..., None] == jnp.arange(NBETA, dtype=jnp.int32)
    first = jnp.min(jnp.where(is_owner, local_id[..., None], col_blocks - 1), axis=(0, 1, 2))
    first_here = jnp.sum(jnp.where(is_owner, first, 0), axis=-1)
    beta_place = owner * FROM_B + (local_id != first_here).astype(jnp.int32)

    order = (x_here - jnp.arange(X, dtype=jnp.int32)) % X
    lists = a_list.reshape(operators, X, Z, row_blocks, slots)
    lists = lax.dynamic_index_in_dim(lists, z_here, 2, keepdims=False)
    counts = a_count.reshape(operators, X, Z, row_blocks)
    counts = lax.dynamic_index_in_dim(counts, z_here, 2, keepdims=False)
    per_x = Z * row_blocks
    here = (slot_ids < counts[..., None]) & (lists // per_x == x_here)
    code = slot_ids * per_x + lists % per_x
    earlier = slot_ids[:, None] > slot_ids
    rank = jnp.sum((here[..., None, :] & earlier).astype(jnp.int32), axis=-1)
    at_rank = here[..., None, :] & (rank[..., None, :] == slot_ids[:, None])
    lists = jnp.sum(jnp.where(at_rank, code[..., None, :], 0), axis=-1)
    sizes = jnp.sum(here.astype(jnp.int32), axis=-1)
    pick = order[:, None] == jnp.arange(X, dtype=jnp.int32)
    lists = jnp.sum(jnp.where(pick[None, :, :, None, None], lists[:, None], 0), axis=2)
    sizes = jnp.sum(jnp.where(pick[None, :, :, None], sizes[:, None], 0), axis=2)
    lists = lists.reshape(operators, X * row_blocks, slots)
    sizes = sizes.reshape(operators, X * row_blocks)

    a_slots = a_blocks.transpose(0, 2, 1, 3)
    b_slots = b_blocks.transpose(0, 2, 1, 3)
    a_half = lax.dynamic_index_in_dim(a_slots, core_here, 0, keepdims=False)
    near = [lax.ppermute(a_half, "alpha", shift_x(d)) for d in (1, 2)]
    a_half, beta_place, beta_counts, lists, sizes = lax.optimization_barrier(
        (a_half, beta_place, beta_counts, lists, sizes)
    )
    near.append(lax.ppermute(a_half, "alpha", shift_x(3)))
    far = [lax.ppermute(part, "beta", SWAP_CORES) for part in near]
    core = core_here.reshape(1)

    c_along_z = lax.all_gather(coeffs, "alpha", axis=0, tiled=True, axis_index_groups=Z_GROUPS)
    sent = pack(wanted, coeffs)
    pool_c = lax.all_to_all(sent, "beta", split_axis=0, concat_axis=0, tiled=True)
    d_one = beta_product(1, beta_place, beta_counts, pool_c, b_slots, (), jnp.bfloat16)
    c_along_z, d_one, near, far = lax.optimization_barrier((c_along_z, d_one, near, far))

    inter_parts = alpha_sums(0, core, lists, sizes, c_along_z, a_slots, near, far)
    sent = sum_pack(wanted, inter_parts)
    pool_inter = lax.all_to_all(sent, "beta", split_axis=0, concat_axis=0, tiled=True)

    d_along_z = lax.all_gather(d_one, "alpha", axis=0, tiled=True, axis_index_groups=Z_GROUPS)
    sigma_here, *sigma_sent = alpha_sums(
        1, core, lists, sizes, d_along_z, a_slots, near, far, after=(sent,)
    )
    sigma = beta_product(0, beta_place, beta_counts, pool_inter, b_slots, (sigma_here,), jnp.float32)
    return fold(sigma, *sigma_sent)


def solution(mesh):
    in_specs = (
        P("alpha", "beta"),
        P(None, "alpha", None, None),
        P(),
        P(),
        P(None, "beta", None, None),
        P(),
        P(),
    )
    return jax.shard_map(
        on_device, mesh=mesh, in_specs=in_specs, out_specs=P("alpha", "beta"), check_vma=False
    )
```

```python
import functools

import jax
import jax.numpy as jnp
from jax import lax
from jax.experimental import pallas as pl
from jax.experimental.pallas import tpu as pltpu
from jax.sharding import PartitionSpec as P

X, Z = 4, 8
Y, CORES = 8, 2
NBETA = Y * CORES
BLK = 128
FROM_B = 2
VMEM_LIMIT = 50 * 1024 * 1024

Z_GROUPS = [[x * Z + z for z in range(Z)] for x in range(X)]
X_GROUPS = [[x * Z + z for x in range(X)] for z in range(Z)]


def shift_x(step):
    return [(x * Z + z, (x + step) % X * Z + z) for x in range(X) for z in range(Z)]


SWAP_CORES = [(y * CORES + c, y * CORES + 1 - c) for y in range(Y) for c in range(CORES)]


def params(limit=VMEM_LIMIT):
    return pltpu.CompilerParams(vmem_limit_bytes=limit)


def pack_kernel(lowest, highest, c_ref, out_ref, blocks, sems):
    for b in range(blocks.shape[0]):
        blocks[b] = c_ref[:, b * BLK : (b + 1) * BLK]

    def each(action):
        for t in range(NBETA * FROM_B):
            action(pltpu.make_async_copy(blocks.at[(lowest, highest)[t % FROM_B][t // FROM_B]], out_ref.at[t], sems.at[t]))

    each(lambda copy: copy.start())
    each(lambda copy: copy.wait())


def pack(wanted, c):
    rows, cols = c.shape
    total = NBETA * FROM_B
    return pl.pallas_call(
        pack_kernel,
        grid_spec=pltpu.PrefetchScalarGridSpec(
            num_scalar_prefetch=2,
            grid=(1,),
            in_specs=[pl.BlockSpec(c.shape, lambda i, low, high: (0, 0))],
            out_specs=pl.BlockSpec(memory_space=pl.ANY),
            scratch_shapes=[
                pltpu.VMEM((cols // BLK, rows, BLK), c.dtype),
                pltpu.SemaphoreType.DMA((total,)),
            ],
        ),
        out_shape=jax.ShapeDtypeStruct((total, rows, BLK), c.dtype),
        compiler_params=params(60 * 1024 * 1024),
        cost_estimate=pl.CostEstimate(flops=0, bytes_accessed=5 << 20, transcendentals=0),
        name="pack",
    )(*wanted, c)


def sum_pack_kernel(lowest, highest, *refs):
    parts, (out_ref, inter, sems) = refs[:-3], refs[-3:]
    step = pl.program_id(0)
    per_step = parts[0].shape[1] // BLK
    for b in range(per_step):
        columns = slice(b * BLK, (b + 1) * BLK)
        total = parts[0][:, columns]
        for part in parts[1:]:
            total += part[:, columns].astype(jnp.float32)
        inter[step * per_step + b] = total.astype(inter.dtype)

    def each(action):
        for t in range(NBETA * FROM_B):
            action(pltpu.make_async_copy(inter.at[(lowest, highest)[t % FROM_B][t // FROM_B]], out_ref.at[t], sems.at[t]))

    @pl.when(step == pl.num_programs(0) - 1)
    def _():
        each(lambda copy: copy.start())
        each(lambda copy: copy.wait())


def sum_pack(wanted, parts, steps=2):
    rows, cols = parts[0].shape
    total = NBETA * FROM_B
    return pl.pallas_call(
        sum_pack_kernel,
        grid_spec=pltpu.PrefetchScalarGridSpec(
            num_scalar_prefetch=2,
            grid=(steps,),
            in_specs=[pl.BlockSpec((rows, cols // steps), lambda i, low, high: (0, i))] * len(parts),
            out_specs=pl.BlockSpec(memory_space=pl.ANY),
            scratch_shapes=[
                pltpu.VMEM((cols // BLK, rows, BLK), jnp.bfloat16),
                pltpu.SemaphoreType.DMA((total,)),
            ],
        ),
        out_shape=jax.ShapeDtypeStruct((total, rows, BLK), jnp.bfloat16),
        compiler_params=params(),
        cost_estimate=pl.CostEstimate(flops=1 << 20, bytes_accessed=6 << 20, transcendentals=0),
        name="sum_pack",
    )(*wanted, *parts)


def beta_kernel(op, place, count, pool_any, b_any, *rest):
    n = len(rest) // 2 - 2
    added_any, out_any, pool_ref, b_ref, added, out_ref, sems = (
        rest[:n],
        rest[n],
        rest[n + 1],
        rest[n + 2],
        rest[n + 3 : 2 * n + 3],
        rest[2 * n + 3],
        rest[2 * n + 4],
    )
    slots, cols, _ = b_ref.shape
    parts = 4
    width = cols // parts

    def factor_copy(i):
        span = pl.ds(i * width, width)
        return pltpu.make_async_copy(
            b_any.at[op, :, span, :], b_ref.at[:, span, :], sems.at[i]
        )

    def out_copy(i):
        span = pl.ds(i * width, width)
        return pltpu.make_async_copy(
            out_ref.at[:, span], out_any.at[:, span], sems.at[parts + i]
        )

    pool_copy = pltpu.make_async_copy(pool_any, pool_ref, sems.at[2 * parts])
    added_copies = [
        pltpu.make_async_copy(added_any[i], added[i], sems.at[2 * parts + 1 + i])
        for i in range(n)
    ]
    pool_copy.start()
    factor_copy(0).start()
    for copy in added_copies:
        copy.start()
    for i in range(1, parts):
        factor_copy(i).start()
    pool_copy.wait()
    for i in range(parts):
        factor_copy(i).wait()
        if i == 0:
            for copy in added_copies:
                copy.wait()
        for block in range(i * width // BLK, (i + 1) * width // BLK):
            columns = slice(block * BLK, (block + 1) * BLK)
            valid = count[op, block]
            picked = [pool_ref[place[op, block, s]] for s in range(slots)]
            factor = [
                jnp.where(s < valid, b_ref[s, columns], jnp.zeros((), b_ref.dtype))
                for s in range(slots)
            ]
            total = lax.dot_general(
                jnp.concatenate(picked, axis=1),
                jnp.concatenate(factor, axis=1),
                (((1,), (1,)), ((), ())),
                preferred_element_type=jnp.float32,
            )
            for part in added:
                total += part[:, columns].astype(jnp.float32)
            out_ref[:, columns] = total.astype(out_ref.dtype)
        out_copy(i).start()
    for i in range(parts):
        out_copy(i).wait()


def beta_product(op, place, count, pool, b_slots, added, dtype):
    _, slots, cols, _ = b_slots.shape
    rows = pool.shape[1]
    anywhere = pl.BlockSpec(memory_space=pl.ANY)
    return pl.pallas_call(
        functools.partial(beta_kernel, op),
        grid_spec=pltpu.PrefetchScalarGridSpec(
            num_scalar_prefetch=2,
            grid=(1,),
            in_specs=[
                anywhere,
                pl.BlockSpec(memory_space=pltpu.HBM),
                *([anywhere] * len(added)),
            ],
            out_specs=anywhere,
            scratch_shapes=[
                pltpu.VMEM(pool.shape, pool.dtype),
                pltpu.VMEM((slots, cols, BLK), b_slots.dtype),
                *[pltpu.VMEM(part.shape, part.dtype) for part in added],
                pltpu.VMEM((rows, cols), dtype),
                pltpu.SemaphoreType.DMA((9 + len(added),)),
            ],
        ),
        out_shape=jax.ShapeDtypeStruct((rows, cols), dtype),
        compiler_params=params(),
        cost_estimate=pl.CostEstimate(
            flops=2 * rows * cols * slots * BLK, bytes_accessed=7 << 20, transcendentals=0
        ),
        name="beta_product",
    )(place, count, pool, b_slots, *added)


FEW = 6


def alpha_kernel(op, steps, core, lists, sizes, pool_any, own, *rest):
    near, far = rest[: X - 1], rest[X - 1 : 2 * (X - 1)]
    outs = rest[-len(steps) - 6 : -6]
    factors, listed_blocks, results, factor_sems, block_sems, out_sems = rest[-6:]
    row_count, slots, _, _ = factors.shape
    blocks = row_count // len(steps)
    pool_blocks = pool_any.shape[0]

    def out_copy(i):
        return pltpu.make_async_copy(results[i], outs[i], out_sems.at[i])

    def fetch(source, i):
        for b in range(blocks):
            listed, row = steps[i] * blocks + b, i * blocks + b

            def start(q, carry):
                code = lists[op, listed, q]
                pltpu.make_async_copy(
                    pool_any.at[code % pool_blocks],
                    listed_blocks.at[row, q],
                    block_sems.at[row, q],
                ).start()
                pltpu.make_async_copy(
                    source.at[code // pool_blocks, pl.ds(b * BLK, BLK), :],
                    factors.at[row, q],
                    factor_sems.at[row, q],
                ).start()
                return carry

            lax.fori_loop(0, sizes[op, listed], start, 0)

    @pl.when(core[0] == op)
    def _():
        for i, t in enumerate(steps):
            if t:
                fetch(near[t - 1], i)

    @pl.when(core[0] != op)
    def _():
        for i, t in enumerate(steps):
            if t:
                fetch(far[t - 1], i)

    for i, t in enumerate(steps):
        if not t:
            fetch(own.at[op], i)
    largest = jnp.int32(0)
    for row in range(row_count):
        listed = steps[row // blocks] * blocks + row % blocks

        def arrive(q, carry):
            pltpu.make_async_copy(
                own.at[op, 0, pl.ds(0, BLK), :], factors.at[row, q], factor_sems.at[row, q]
            ).wait()
            pltpu.make_async_copy(
                pool_any.at[0], listed_blocks.at[row, q], block_sems.at[row, q]
            ).wait()
            return carry

        lax.fori_loop(0, sizes[op, listed], arrive, 0)
        largest = jnp.maximum(largest, sizes[op, listed])

    def multiply(depth):
        for i, t in enumerate(steps):
            for b in range(blocks):
                listed, row = t * blocks + b, i * blocks + b
                size = sizes[op, listed]
                left = [
                    jnp.where(q < size, factors[row, q], jnp.zeros((), factors.dtype))
                    for q in range(depth)
                ]
                right = [
                    jnp.where(
                        q < size, listed_blocks[row, q], jnp.zeros((), listed_blocks.dtype)
                    )
                    for q in range(depth)
                ]
                total = jnp.dot(
                    jnp.concatenate(left, axis=1),
                    jnp.concatenate(right, axis=0),
                    preferred_element_type=jnp.float32,
                )
                results[i][b * BLK : (b + 1) * BLK, :] = total.astype(results[i].dtype)
            out_copy(i).start()

    @pl.when(largest <= FEW)
    def _():
        multiply(FEW)

    @pl.when(largest > FEW)
    def _():
        multiply(slots)

    for i in range(len(steps)):
        out_copy(i).wait()


def alpha_products(op, steps, core, lists, sizes, gathered, own, near, far, after):
    _, slots, rows, _ = own.shape
    cols = gathered.shape[1]
    pool = gathered.reshape(gathered.shape[0] // BLK, BLK, cols)
    operands = [own, *near, *far, *after]
    row_count = len(steps) * rows // BLK
    anywhere = pl.BlockSpec(memory_space=pl.ANY)
    types = [jnp.bfloat16 if t else jnp.float32 for t in steps]
    return pl.pallas_call(
        functools.partial(alpha_kernel, op, steps),
        grid_spec=pltpu.PrefetchScalarGridSpec(
            num_scalar_prefetch=3,
            grid=(1,),
            in_specs=[anywhere] * (1 + len(operands)),
            out_specs=[anywhere] * len(steps),
            scratch_shapes=[
                pltpu.VMEM((row_count, slots, BLK, BLK), own.dtype),
                pltpu.VMEM((row_count, slots, BLK, cols), pool.dtype),
                [pltpu.VMEM((rows, cols), kind) for kind in types],
                pltpu.SemaphoreType.DMA((row_count, slots)),
                pltpu.SemaphoreType.DMA((row_count, slots)),
                pltpu.SemaphoreType.DMA((len(steps),)),
            ],
        ),
        out_shape=[jax.ShapeDtypeStruct((rows, cols), kind) for kind in types],
        compiler_params=params(),
        cost_estimate=pl.CostEstimate(
            flops=rows * cols * slots * BLK, bytes_accessed=12 << 20, transcendentals=0
        ),
        name="alpha_products",
    )(core, lists, sizes, pool, *operands)


def alpha_sums(op, core, lists, sizes, gathered, own, near, far, after=()):
    common = (core, lists, sizes, gathered, own, near, far)
    (across,) = alpha_products(op, (2,), *common, after)
    after_one, before_one = alpha_products(op, (1, 3), *common, (across,))
    (here,) = alpha_products(op, (0,), *common, (after_one,))
    from_across = lax.ppermute(across, "alpha", shift_x(X - 2))
    sent = [
        lax.ppermute(part, "alpha", shift_x(X - d)) for d, part in ((1, after_one), (3, before_one))
    ]
    return [fold(here, from_across), *sent]


def fold_kernel(first_ref, *refs):
    total = first_ref[...]
    for ref in refs[:-1]:
        total += ref[...].astype(jnp.float32)
    refs[-1][...] = total


def fold(first, *others):
    rows, cols = first.shape
    by_rows = pl.BlockSpec((rows // 2, cols), lambda i: (i, 0))
    return pl.pallas_call(
        fold_kernel,
        grid=(2,),
        in_specs=[by_rows] * (1 + len(others)),
        out_specs=by_rows,
        out_shape=jax.ShapeDtypeStruct(first.shape, jnp.float32),
        compiler_params=params(),
        cost_estimate=pl.CostEstimate(flops=1 << 20, bytes_accessed=48 << 20, transcendentals=0),
        name="fold",
    )(first, *others)


def on_device(coeffs, a_blocks, a_list, a_count, b_blocks, b_list, b_count):
    operators, local_rows, slots, _ = a_blocks.shape
    local_cols = coeffs.shape[1]
    row_blocks = local_rows // BLK
    col_blocks = local_cols // BLK
    alpha_here = lax.axis_index("alpha")
    beta_here = lax.axis_index("beta")
    x_here = alpha_here // Z
    z_here = alpha_here % Z
    core_here = beta_here % CORES
    slot_ids = jnp.arange(slots, dtype=jnp.int32)

    local = b_list.reshape(operators, NBETA, col_blocks * slots) - beta_here * col_blocks
    inside = (local >= 0) & (local < col_blocks)
    lowest = jnp.min(jnp.where(inside, local, col_blocks - 1), axis=(0, 2))
    highest = jnp.max(jnp.where(inside, local, 0), axis=(0, 2))
    wanted = (lowest, highest)

    mine = lax.dynamic_slice_in_dim(b_list, beta_here * col_blocks, col_blocks, 1)
    beta_counts = lax.dynamic_slice_in_dim(b_count, beta_here * col_blocks, col_blocks, 1)
    owner = mine // col_blocks
    local_id = mine % col_blocks
    is_owner = owner[..., None] == jnp.arange(NBETA, dtype=jnp.int32)
    first = jnp.min(jnp.where(is_owner, local_id[..., None], col_blocks - 1), axis=(0, 1, 2))
    first_here = jnp.sum(jnp.where(is_owner, first, 0), axis=-1)
    beta_place = owner * FROM_B + (local_id != first_here).astype(jnp.int32)

    order = (x_here - jnp.arange(X, dtype=jnp.int32)) % X
    lists = a_list.reshape(operators, X, Z, row_blocks, slots)
    lists = lax.dynamic_index_in_dim(lists, z_here, 2, keepdims=False)
    counts = a_count.reshape(operators, X, Z, row_blocks)
    counts = lax.dynamic_index_in_dim(counts, z_here, 2, keepdims=False)
    per_x = Z * row_blocks
    here = (slot_ids < counts[..., None]) & (lists // per_x == x_here)
    code = slot_ids * per_x + lists % per_x
    earlier = slot_ids[:, None] > slot_ids
    rank = jnp.sum((here[..., None, :] & earlier).astype(jnp.int32), axis=-1)
    at_rank = here[..., None, :] & (rank[..., None, :] == slot_ids[:, None])
    lists = jnp.sum(jnp.where(at_rank, code[..., None, :], 0), axis=-1)
    sizes = jnp.sum(here.astype(jnp.int32), axis=-1)
    pick = order[:, None] == jnp.arange(X, dtype=jnp.int32)
    lists = jnp.sum(jnp.where(pick[None, :, :, None, None], lists[:, None], 0), axis=2)
    sizes = jnp.sum(jnp.where(pick[None, :, :, None], sizes[:, None], 0), axis=2)
    lists = lists.reshape(operators, X * row_blocks, slots)
    sizes = sizes.reshape(operators, X * row_blocks)

    a_slots = a_blocks.transpose(0, 2, 1, 3)
    b_slots = b_blocks.transpose(0, 2, 1, 3)
    a_half = lax.dynamic_index_in_dim(a_slots, core_here, 0, keepdims=False)
    near = [lax.ppermute(a_half, "alpha", shift_x(d)) for d in (1, 2)]
    a_half, beta_place, beta_counts, lists, sizes = lax.optimization_barrier(
        (a_half, beta_place, beta_counts, lists, sizes)
    )
    near.append(lax.ppermute(a_half, "alpha", shift_x(3)))
    far = [lax.ppermute(part, "beta", SWAP_CORES) for part in near]
    core = core_here.reshape(1)

    c_along_z = lax.all_gather(coeffs, "alpha", axis=0, tiled=True, axis_index_groups=Z_GROUPS)
    sent = pack(wanted, coeffs)
    pool_c = lax.all_to_all(sent, "beta", split_axis=0, concat_axis=0, tiled=True)
    d_one = beta_product(1, beta_place, beta_counts, pool_c, b_slots, (), jnp.bfloat16)
    c_along_z, d_one, near, far = lax.optimization_barrier((c_along_z, d_one, near, far))

    inter_parts = alpha_sums(0, core, lists, sizes, c_along_z, a_slots, near, far)
    sent = sum_pack(wanted, inter_parts)
    pool_inter = lax.all_to_all(sent, "beta", split_axis=0, concat_axis=0, tiled=True)

    d_along_z = lax.all_gather(d_one, "alpha", axis=0, tiled=True, axis_index_groups=Z_GROUPS)
    sigma_here, *sigma_sent = alpha_sums(
        1, core, lists, sizes, d_along_z, a_slots, near, far, after=(sent,)
    )
    sigma = beta_product(0, beta_place, beta_counts, pool_inter, b_slots, (sigma_here,), jnp.float32)
    return fold(sigma, *sigma_sent)


def solution(mesh):
    in_specs = (
        P("alpha", "beta"),
        P(None, "alpha", None, None),
        P(),
        P(),
        P(None, "beta", None, None),
        P(),
        P(),
    )
    return jax.shard_map(
        on_device, mesh=mesh, in_specs=in_specs, out_specs=P("alpha", "beta"), check_vma=False
    )
```
